32 devices in a mesh: job: 2 (over x), fsdp: 8 (over z, y), replica: 2 (over core).
Axes of the slice: x: 2, y: 2, z: 4, core: 2. Of those that a mesh axis runs over, the one named last changes fastest.
Arguments:
- tokens: bfloat16 [4, 2, 1152, 2048], P(('job', 'replica'), None, 'fsdp'), parts along dimension 0, may hold values from -6 to 6
- queries: bfloat16 [4, 2, 1152, 2048], P(('job', 'replica'), None, 'fsdp'), parts along dimension 0, may hold values from -64 to 64
- targets: bfloat16 [4, 2, 1152, 2048], P(('job', 'replica'), None, 'fsdp'), parts along dimension 0, may hold values from -6 to 6
- gain: float32 [2048], replicated, may hold values from 0.5 to 1.5
- base: float32 [4096, 1024], P(('job', 'fsdp')), parts along dimension 0, may hold values from -4 to 4
- offset: float32 [2, 4096, 1024], P('replica', ('job', 'fsdp')), parts along dimension 1, may hold values from -3 to 3
- first_moment: float32 [2, 4096, 1024], P('replica', ('job', 'fsdp')), parts along dimension 1, may hold values from -0.0014648438 to 0.0014648438
- second_moment: float32 [2, 4096, 1024], P('replica', ('job', 'fsdp')), parts along dimension 1, may hold values from 1e-09 to 1e-06
- outer_momentum: float32 [4096, 1024], P(('job', 'fsdp')), parts along dimension 0, may hold values from -1.5 to 1.5
- exponents: int32 [4096, 8], P(('job', 'fsdp')), parts along dimension 0, may hold values from -12 to -6
Outputs:
- new_base: float32 [4096, 1024], P(('job', 'fsdp')), parts along dimension 0
- new_momentum: float32 [4096, 1024], P(('job', 'fsdp')), parts along dimension 0
The draws below stay inside these ranges and needn't reach their ends.
There are 2 independent parts, one for each index of `job`. The reference program is written for one: setup_inputs(seed, part) draws one part's arguments, and reference() takes and returns one part's arrays. A program takes and returns all parts, laid end to end along the dimension named above; an argument that names none is the same for every part. Nothing has to cross between parts.
All inputs are finite; a program needn't handle non-finite values.
Results may differ from the reference program's by a relative error of at most 0.024.
Values may be sent and summed in bfloat16 or wider, within the bound.
A program may use at most 64 MiB of HBM per device.

```python
import math
import jax
import jax.numpy as jnp
from jax import lax

D = 2048
HEADS = 32
KV_HEADS = 8
HEAD = 64
TOK_DEV = 144
STEPS = 2
BLOCK = 128
QD = 2048
KVD = 512
REPLICAS = 2
TOK_R = 1152


def draw_queries(key, part):
    key = jax.random.fold_in(key, 11)
    shape = (REPLICAS, STEPS, TOK_R, QD)
    first = jax.random.fold_in(key, 0)
    values = jnp.clip(jax.random.normal(first, shape, jnp.float32), -6.0, 6.0)
    return values.astype(jnp.bfloat16)


def with_ends(values, rng, least, top_value):
    longest = values.shape.index(max(values.shape))
    spots = []
    for shift in (0, 1):
        where = [jax.random.randint(jax.random.fold_in(rng, axis), (), 0, length) for axis, length in enumerate(values.shape)]
        where[longest] = (where[longest] + shift) % values.shape[longest]
        spots.append(tuple(where))
    return values.at[spots[0]].set(least).at[spots[1]].set(top_value)


def steps_of(key, dims, shards, smallest, top_value):
    level = 1.0
    for dim, parts in shards:
        heights = jax.random.uniform(jax.random.fold_in(jax.random.fold_in(key, 6), dim), (parts,), jnp.float32, smallest / len(shards), top_value / len(shards))
        level = level * jnp.repeat(jnp.exp(heights), dims[dim] // parts).reshape((-1,) + (1,) * (len(dims) - 1 - dim))
    return level


def centred(rng, extent, spread, most, cuts=(), kind=jnp.bfloat16):
    level = steps_of(rng, extent, cuts, -0.22, 0.18) if cuts else 1.0
    drawn = jax.random.normal(rng, extent, jnp.float32) * spread * level
    return jnp.minimum(jnp.maximum(drawn, -most), most).astype(kind)


def setup_inputs(seed: int = 0, part: int = 0) -> dict:
    key_of = jax.random.split(jax.random.key(seed), 11)
    part_keys = jax.random.split(jax.random.fold_in(key_of[10], part), 11)
    tokens = centred(part_keys[0], (REPLICAS, STEPS, TOK_R, D), 1.0, 6.0, ((0, 2), (2, 8)))
    queries = draw_queries(jax.random.fold_in(jax.random.fold_in(key_of[10], part), 71), part)
    targets = centred(part_keys[2], (REPLICAS, STEPS, TOK_R, QD), 1.0, 6.0, ((0, 2), (2, 8)))
    gain = jnp.clip(1.0 + 0.1 * jax.random.normal(key_of[3], (D,), jnp.float32), 0.5, 1.5)
    base = centred(part_keys[4], (D, 2 * KVD), 1.0, 4.0, ((0, 8),), jnp.float32)
    offset = centred(part_keys[5], (REPLICAS, D, 2 * KVD), 0.2, 3.0, ((0, 2), (1, 8)), jnp.float32)
    first_moment = centred(part_keys[6], (REPLICAS, D, 2 * KVD), 0.0001, 0.0014648438, ((0, 2), (1, 8)), jnp.float32)
    second_moment = jnp.clip(jnp.exp(math.log(9.999999974752427e-07) - 6.9077553 * jax.random.uniform(part_keys[7], (REPLICAS, D, 2 * KVD), jnp.float32) ** steps_of(part_keys[7], (REPLICAS, D, 2 * KVD), ((0, 2), (1, 8)), -0.2, 0.2)), 9.999999717180685e-10, 9.999999974752427e-07)
    outer_momentum = centred(part_keys[8], (D, 2 * KVD), 0.1, 1.5, ((0, 8),), jnp.float32)
    exponents = with_ends(jax.random.randint(part_keys[9], (D, 2 * KVD // BLOCK), -12, -5), jax.random.fold_in(part_keys[9], 1), -12, (-5) - 1).astype(jnp.int32)
    return {"tokens": tokens, "queries": queries, "targets": targets, "gain": gain, "base": base, "offset": offset, "first_moment": first_moment, "second_moment": second_moment, "outer_momentum": outer_momentum, "exponents": exponents}


def normalize(hidden, gain):
    values = hidden.astype(jnp.float32)
    power = lax.optimization_barrier(jnp.mean(values * values, axis=-1, keepdims=True))
    return (values * lax.rsqrt(power + 1e-05) * gain).astype(jnp.bfloat16)

def sequence_grad(query, keyval, target, tok_total):
    length = query.shape[0]
    group = HEADS // KV_HEADS
    scale = HEAD ** (-0.5)
    qh = query.reshape(length, KV_HEADS, group, HEAD).astype(jnp.float32)
    keys = keyval[:, :KVD].reshape(length, KV_HEADS, HEAD).astype(jnp.float32)
    values = keyval[:, KVD:].reshape(length, KV_HEADS, HEAD).astype(jnp.float32)
    scores = jnp.einsum('qhgd,khd->hgqk', qh, keys) * scale
    causal = jnp.arange(length)[:, None] >= jnp.arange(length)[None, :]
    scores = jnp.where(causal, scores, -1e+30)
    top = lax.optimization_barrier(jnp.max(scores, axis=-1, keepdims=True))
    expo = jnp.exp(scores - top)
    probs = expo / lax.optimization_barrier(jnp.sum(expo, axis=-1, keepdims=True))
    probs_b = probs.astype(jnp.bfloat16).astype(jnp.float32)
    output = jnp.einsum('hgqk,khd->qhgd', probs_b, values)
    goal = target.reshape(length, KV_HEADS, group, HEAD).astype(jnp.float32)
    grad_out = ((output - goal) / tok_total).astype(jnp.bfloat16).astype(jnp.float32)
    grad_v = jnp.einsum('hgqk,qhgd->khd', probs_b, grad_out)
    grad_p = jnp.einsum('qhgd,khd->hgqk', grad_out, values)
    grad_s = probs * (grad_p - lax.optimization_barrier(jnp.sum(probs * grad_p, axis=-1, keepdims=True)))
    grad_sb = (grad_s * scale).astype(jnp.bfloat16).astype(jnp.float32)
    grad_k = jnp.einsum('hgqk,qhgd->khd', grad_sb, qh)
    joined = jnp.concatenate([grad_k.reshape(length, KVD), grad_v.reshape(length, KVD)], axis=1)
    return (joined * D ** (-0.5)).astype(jnp.bfloat16)

def adam_update(weights, mom1, mom2, grad):
    mom1 = 0.9 * mom1 + 0.1 * grad
    mom2 = 0.95 * mom2 + 0.05 * grad * grad
    weights = weights - 0.08 * (mom1 / (jnp.sqrt(mom2) + 1e-08) + 0.01 * weights)
    return (weights, mom1, mom2)

def sequence_sum(normed, grad_kv):
    count = TOK_R // TOK_DEV
    seq_n = normed.reshape(count, TOK_DEV, D)
    seq_g = grad_kv.reshape(count, TOK_DEV, 2 * KVD)

    def add_part(total, item):
        part = jnp.dot(item[0].T, item[1], preferred_element_type=jnp.float32)
        rounded = lax.optimization_barrier(part.astype(jnp.bfloat16)).astype(jnp.float32)
        return (total + rounded, None)
    total, _ = lax.scan(add_part, jnp.zeros((D, 2 * KVD), jnp.float32), (seq_n, seq_g))
    return total

def reference(tokens, queries, targets, gain, base, offset, first_moment, second_moment, outer_momentum, exponents):
    rows = base.shape[0]
    blocks = exponents.shape[1]
    scale = jnp.exp2(exponents.astype(jnp.float32))[:, :, None]
    total = jnp.zeros((rows, blocks, BLOCK), jnp.float32)
    for rep in range(REPLICAS):
        weights = base + offset[rep]
        mom1 = first_moment[rep]
        mom2 = second_moment[rep]
        for step in range(STEPS):
            normed = normalize(tokens[rep, step], gain)
            wide = weights.astype(jnp.bfloat16)
            keyval = (jnp.dot(normed, wide, preferred_element_type=jnp.float32) * D ** (-0.5)).astype(jnp.bfloat16)
            seq_q = queries[rep, step].reshape(TOK_R // TOK_DEV, TOK_DEV, QD)
            seq_kv = keyval.reshape(TOK_R // TOK_DEV, TOK_DEV, 2 * KVD)
            seq_t = targets[rep, step].reshape(TOK_R // TOK_DEV, TOK_DEV, QD)
            grads = lax.map(lambda item: sequence_grad(item[0], item[1], item[2], TOK_R), (seq_q, seq_kv, seq_t))
            grad_kv = grads.reshape(TOK_R, 2 * KVD)
            grad = sequence_sum(normed, grad_kv)
            weights, mom1, mom2 = adam_update(weights, mom1, mom2, grad)
        delta = (base - weights).reshape(rows, blocks, BLOCK)
        coded = jnp.clip(delta / scale, -448.0, 448.0).astype(jnp.bfloat16)
        total = total + coded.astype(jnp.float32)
    average = (total * scale / REPLICAS).reshape(rows, blocks * BLOCK)
    new_momentum = 0.9 * outer_momentum + average
    new_base = base - 0.7 * (0.9 * new_momentum + average)
    return (new_base, new_momentum)
```

```python
import functools

import jax
import jax.numpy as jnp
from jax import lax
from jax.experimental import pallas as pl
from jax.experimental.pallas import tpu as pltpu
from jax.sharding import PartitionSpec as P

D = 2048
HEADS = 32
KV_HEADS = 8
HEAD = 64
CHUNKS = 4
GROUP = HEADS // KV_HEADS
KVD = KV_HEADS * HEAD
HALF = KVD // CHUNKS
WIDE = 2 * HALF
MESH = pl.DeviceIdType.MESH


def ring_device(place, n):
    place = lax.rem(place + 2 * n, n)
    if n != 8:
        return place
    return jnp.where(place < n // 2, 2 * place, 2 * n - 1 - 2 * place)


def ring_place(device, n):
    if n != 8:
        return device
    return jnp.where(lax.rem(device, 2) == 0, device // 2, n - 1 - device // 2)


def columns(c, half):
    return slice(half * KVD + c * HALF, half * KVD + (c + 1) * HALF)


def head_grads(qs, ts, kv, tok_total):
    length = kv.shape[0]
    keys, vals = [], []
    row = lax.broadcasted_iota(jnp.int32, (length, length), 0)
    col = lax.broadcasted_iota(jnp.int32, (length, length), 1)
    causal = jnp.concatenate([row >= col] * GROUP, axis=0)
    nt = (((1,), (1,)), ((), ()))
    tn = (((0,), (0,)), ((), ()))
    for j in range(HALF // HEAD):
        k = kv[:, j * HEAD : (j + 1) * HEAD]
        v = kv[:, HALF + j * HEAD : HALF + (j + 1) * HEAD]
        heads = [slice((j * GROUP + i) * HEAD, (j * GROUP + i + 1) * HEAD) for i in range(GROUP)]
        q = jnp.concatenate([qs[:, h] for h in heads], axis=0)
        goal = jnp.concatenate([ts[:, h] for h in heads], axis=0).astype(jnp.float32)
        scores = lax.dot_general(q, k, nt, preferred_element_type=jnp.float32) * HEAD ** (-0.5)
        scores = jnp.where(causal, scores, -1e30)
        top = jnp.max(scores, axis=-1, keepdims=True)
        expo = jnp.exp(scores - top)
        probs = expo * (1.0 / jnp.sum(expo, axis=-1, keepdims=True))
        probs_b = probs.astype(jnp.bfloat16)
        out = jnp.dot(probs_b, v, preferred_element_type=jnp.float32)
        grad_out = ((out - goal) * (1.0 / tok_total)).astype(jnp.bfloat16)
        grad_v = lax.dot_general(probs_b, grad_out, tn, preferred_element_type=jnp.float32)
        grad_p = lax.dot_general(grad_out, v, nt, preferred_element_type=jnp.float32)
        inner = jnp.sum(probs * grad_p, axis=-1, keepdims=True)
        grad_sb = (probs * (grad_p - inner) * HEAD ** (-0.5)).astype(jnp.bfloat16)
        grad_k = lax.dot_general(grad_sb, q, tn, preferred_element_type=jnp.float32)
        keys.append(grad_k)
        vals.append(grad_v)
    joined = jnp.concatenate(keys + vals, axis=1)
    return (joined * D ** (-0.5)).astype(jnp.bfloat16)


def kernel(
    n, tok_total,
    tok_ref, gain_ref, base_ref, off_ref, inv_ref, q_hbm, t_hbm, m_hbm, v_hbm,
    out_ref,
    q_ref, t_ref, m_ref, v_ref, w_ref, wall, gall, nsend, cols, kvacc, gacc, coded,
    load_sem, w_send, w_recv, g_send, g_recv, a_send, a_recv, c_send, c_recv,
):
    me = lax.axis_index("fsdp")
    rep = lax.axis_index("replica")
    place = ring_place(me, n)
    near = (ring_device(place + 1, n), ring_device(place - 1, n))
    steps = tok_ref.shape[0]
    rows = base_ref.shape[0]
    last = n // 2

    barrier = pltpu.get_barrier_semaphore()
    for k in range(1, n):
        pl.semaphore_signal(barrier, inc=1, device_id={"fsdp": lax.rem(me + k, n)}, device_id_type=MESH)
    pl.semaphore_signal(barrier, inc=1, device_id={"replica": 1 - rep}, device_id_type=MESH)

    loads = [
        pltpu.make_async_copy(src, dst, load_sem.at[i])
        for i, (src, dst) in enumerate(((q_hbm, q_ref), (t_hbm, t_ref), (m_hbm, m_ref), (v_hbm, v_ref)))
    ]
    for load in loads:
        load.start()

    def put_wide(s, c, half, w):
        wall[s, me, c, :, half * HALF : (half + 1) * HALF] = w.astype(jnp.bfloat16)

    for c in range(CHUNKS):
        for half in (0, 1):
            w = base_ref[:, columns(c, half)] + off_ref[:, columns(c, half)]
            w_ref[:, columns(c, half)] = w
            put_wide(0, c, half, w)

    pl.semaphore_wait(barrier, n)

    sends = []

    def hop_copy(buf, send, recv, s, c, d, h, owner):
        return pltpu.make_async_remote_copy(
            src_ref=buf.at[s, owner, c], dst_ref=buf.at[s, owner, c],
            send_sem=send.at[s, c, d, h], recv_sem=recv.at[s, c, d, h],
            device_id={"fsdp": near[d]}, device_id_type=MESH,
        )

    def ring_start(ring, s, c):
        for d in (0, 1):
            copy = hop_copy(*ring, s, c, d, 0, me)
            copy.start()
            sends.append(copy)

    def ring_hop(ring, s, c, h):
        owners = []
        for d in (0, 1):
            if h == last and d != c % 2:
                continue
            owner = ring_device(place - h if d == 0 else place + h, n)
            hop_copy(*ring, s, c, d, h - 1, owner).wait_recv()
            if h < last - 1 or (h == last - 1 and d == c % 2):
                copy = hop_copy(*ring, s, c, d, h, owner)
                copy.start()
                sends.append(copy)
            owners.append(owner)
        return owners

    w_ring = (wall, w_send, w_recv)
    g_ring = (gall, g_send, g_recv)
    tn = (((0,), (0,)), ((), ()))

    for c in range(CHUNKS):
        ring_start(w_ring, 0, c)

    for s in range(steps):
        values = tok_ref[s].astype(jnp.float32)
        power = jnp.mean(values * values, axis=-1, keepdims=True)
        normed = (values * lax.rsqrt(power + 1e-05) * gain_ref[...]).astype(jnp.bfloat16)
        for p in range(n):
            nsend[s, p] = normed[:, p * rows : (p + 1) * rows]
        cols[s, me] = nsend[s, me]

    def swap_copy(s, k):
        to = lax.rem(me + k, n)
        return pltpu.make_async_remote_copy(
            src_ref=nsend.at[s, to], dst_ref=cols.at[s, me],
            send_sem=a_send.at[s, k], recv_sem=a_recv.at[s, k],
            device_id={"fsdp": to}, device_id_type=MESH,
        )

    def kv_add(s, c, owner, first=False):
        part = jnp.dot(nsend[s, owner], wall[s, owner, c], preferred_element_type=jnp.float32)
        kvacc[c] = part if first else kvacc[c] + part

    def grad_add(s, c, owner, first=False):
        part = lax.dot_general(cols[s, owner], gall[s, owner, c], tn, preferred_element_type=jnp.float32)
        part = part.astype(jnp.bfloat16).astype(jnp.float32)
        gacc[c] = part if first else gacc[c] + part

    def attend(s, c):
        kv = (kvacc[c] * D ** (-0.5)).astype(jnp.bfloat16)
        span = slice(c * GROUP * HALF, (c + 1) * GROUP * HALF)
        gall[s, me, c] = head_grads(q_ref[s, :, span], t_ref[s, :, span], kv, tok_total)

    def code_copy(c):
        return pltpu.make_async_remote_copy(
            src_ref=coded.at[0, c], dst_ref=coded.at[1, c],
            send_sem=c_send.at[c], recv_sem=c_recv.at[c],
            device_id={"replica": 1 - rep}, device_id_type=MESH,
        )

    def adam(s, c):
        for half in (0, 1):
            at = columns(c, half)
            inside = slice(half * HALF, (half + 1) * HALF)
            grad = gacc[c, :, inside]
            mom1 = 0.9 * m_ref[:, at] + 0.1 * grad
            mom2 = 0.95 * v_ref[:, at] + 0.05 * grad * grad
            w = w_ref[:, at]
            w = w - 0.08 * (mom1 / (jnp.sqrt(mom2) + 1e-08) + 0.01 * w)
            if s < steps - 1:
                m_ref[:, at] = mom1
                v_ref[:, at] = mom2
                w_ref[:, at] = w
                put_wide(s + 1, c, half, w)
            else:
                block = half * CHUNKS + c
                delta = (base_ref[:, at] - w) * inv_ref[:, block : block + 1]
                coded[0, c, :, inside] = jnp.clip(delta, -448.0, 448.0).astype(jnp.bfloat16)

    for s in range(steps):
        for c in range(CHUNKS):
            kv_add(s, c, me, True)
        for h in range(1, last + 1):
            for c in range(CHUNKS):
                for owner in ring_hop(w_ring, s, c, h):
                    kv_add(s, c, owner)
        for k in range(1, n):
            copy = swap_copy(s, k)
            copy.start()
            sends.append(copy)
        if s == 0:
            for load in loads:
                load.wait()
        for c in range(CHUNKS):
            attend(s, c)
            ring_start(g_ring, s, c)
        for c in range(CHUNKS):
            grad_add(s, c, me, True)
        for k in range(1, n):
            pltpu.make_async_remote_copy(
                src_ref=nsend.at[s, me], dst_ref=cols.at[s, lax.rem(me - k + n, n)],
                send_sem=a_send.at[s, k], recv_sem=a_recv.at[s, k],
                device_id={"fsdp": lax.rem(me + k, n)}, device_id_type=MESH,
            ).wait_recv()
        for h in range(1, last + 1):
            for c in range(CHUNKS):
                for owner in ring_hop(g_ring, s, c, h):
                    grad_add(s, c, owner)
        for c in range(CHUNKS):
            adam(s, c)
            if s < steps - 1:
                ring_start(w_ring, s + 1, c)
            else:
                copy = code_copy(c)
                copy.start()
                sends.append(copy)
    for c in range(CHUNKS):
        code_copy(c).wait_recv()
        for half in (0, 1):
            inside = slice(half * HALF, (half + 1) * HALF)
            out_ref[:, columns(c, half)] = (
                coded[0, c, :, inside].astype(jnp.float32) + coded[1, c, :, inside].astype(jnp.float32)
            )
    for copy in sends:
        copy.wait_send()


def shards(
    n, replicas,
    tokens, queries, targets, gain, base, offset,
    first_moment, second_moment, outer_momentum, exponents,
):
    rows, width = base.shape
    steps, length = tokens.shape[1], tokens.shape[2]
    blocks = exponents.shape[1]
    block_len = width // blocks
    scale = jnp.exp2(exponents.astype(jnp.float32))
    bf, f32 = jnp.bfloat16, jnp.float32
    vmem = pl.BlockSpec(memory_space=pltpu.VMEM)
    hbm = pl.BlockSpec(memory_space=pl.ANY)
    hops = n // 2
    dma = pltpu.SemaphoreType.DMA
    total = pl.pallas_call(
        functools.partial(kernel, n, length * n),
        out_shape=jax.ShapeDtypeStruct((rows, width), f32),
        in_specs=[vmem] * 5 + [hbm] * 4,
        out_specs=vmem,
        scratch_shapes=[
            pltpu.VMEM(queries.shape[1:], bf),
            pltpu.VMEM(targets.shape[1:], bf),
            pltpu.VMEM((rows, width), f32),
            pltpu.VMEM((rows, width), f32),
            pltpu.VMEM((rows, width), f32),
            pltpu.VMEM((steps, n, CHUNKS, rows, WIDE), bf),
            pltpu.VMEM((steps, n, CHUNKS, length, WIDE), bf),
            pltpu.VMEM((steps, n, length, rows), bf),
            pltpu.VMEM((steps, n, length, rows), bf),
            pltpu.VMEM((CHUNKS, length, WIDE), f32),
            pltpu.VMEM((CHUNKS, rows, WIDE), f32),
            pltpu.VMEM((2, CHUNKS, rows, WIDE), bf),
            dma((4,)),
            dma((steps, CHUNKS, 2, hops)),
            dma((steps, CHUNKS, 2, hops)),
            dma((steps, CHUNKS, 2, hops)),
            dma((steps, CHUNKS, 2, hops)),
            dma((steps, n)),
            dma((steps, n)),
            dma((CHUNKS,)),
            dma((CHUNKS,)),
        ],
        compiler_params=pltpu.CompilerParams(
            collective_id=0, has_side_effects=True, vmem_limit_bytes=60 * 2**20
        ),
    )(
        tokens[0], gain[None, :], base, offset[0], 1.0 / scale,
        queries[0], targets[0], first_moment[0], second_moment[0],
    )
    wide_scale = jnp.repeat(scale / replicas, block_len, axis=1)
    average = total * wide_scale
    new_momentum = 0.9 * outer_momentum + average
    new_base = base - 0.7 * (0.9 * new_momentum + average)
    return (new_base, new_momentum)


def solution(mesh):
    in_specs = (
        P(("job", "replica"), None, "fsdp", None),
        P(("job", "replica"), None, "fsdp", None),
        P(("job", "replica"), None, "fsdp", None),
        P(),
        P(("job", "fsdp"), None),
        P("replica", ("job", "fsdp"), None),
        P("replica", ("job", "fsdp"), None),
        P("replica", ("job", "fsdp"), None),
        P(("job", "fsdp"), None),
        P(("job", "fsdp"), None),
    )
    out_specs = (P(("job", "fsdp"), None), P(("job", "fsdp"), None))
    body = functools.partial(shards, mesh.shape["fsdp"], mesh.shape["replica"])
    return jax.shard_map(body, mesh=mesh, in_specs=in_specs, out_specs=out_specs, check_vma=False)
```
